32 devices in a mesh: ctx: 8 (over z, x), tp: 4 (over y, core).
Axes of the slice: x: 2, y: 2, z: 4, core: 2. Of those that a mesh axis runs over, the one named last changes fastest.
Arguments:
- normed_input: bfloat16 [4096, 4096], P('ctx'), may hold values from -12 to 12
- w_query: bfloat16 [4096, 2048], P(None, 'tp'), may hold values from -0.09375 to 0.09375
- key_weight: bfloat16 [4096, 512], P(None, 'tp'), may hold values from -0.09375 to 0.09375
- value_weight: bfloat16 [4096, 512], P(None, 'tp'), may hold values from -0.09375 to 0.09375
- output_weight: bfloat16 [4096, 2048], P(None, 'tp'), may hold values from -0.125 to 0.125
- output_cotangent: bfloat16 [4096, 4096], P('ctx'), may hold values from -6 to 6
- piece_doc: int32 [512], replicated, may hold values from 0 to 31, as said below
- piece_offset: int32 [512], replicated, may hold values from 0 to 480, as said below
- doc_owner: int32 [32], replicated, may hold values from 0 to 7, as said below
Outputs:
- grad_in: bfloat16 [4096, 4096], P('ctx', 'tp')
- grad_query: bfloat16 [4096, 2048], P('ctx', 'tp')
- grad_key: bfloat16 [4096, 512], P('ctx', 'tp')
- grad_value: bfloat16 [4096, 512], P('ctx', 'tp')
- grad_out: bfloat16 [4096, 2048], P('ctx', 'tp')
The draws below stay inside these ranges and needn't reach their ends.
Inputs may be any that keep to these rules, and one draw needn't show every extreme that they name: `piece_doc`: every document has at least one piece; the pieces of one document, in increasing token order, have offsets 0, 8, 16 and so on. `piece_offset`: A piece belongs to the owner of its document. The pieces of the tokens of one index of ctx go to exactly 8 / 2 owners, exactly 128 tokens to each of them; so every owner receives 512 tokens. `doc_owner`: every device of ctx owns exactly 4 documents.
All inputs are finite; a program needn't handle non-finite values.
Results may differ from the reference program's by a relative error of at most 0.015.
Values may be sent and summed in bfloat16 or wider, within the bound.
A program may use at most 128 MiB of HBM per device.

```python
import math
import jax
import jax.numpy as jnp
from jax import lax

MODEL_WIDTH = 4096
QUERY_HEAD_COUNT = 16
KV_HEAD_COUNT = 4
HEAD_SIZE = 128
PIECE = 8
DOCS_OWN = 4
TOKENS_PER_SHARD = 512
TOKENS = 4096
SLOTS = 128
NDOC = 32
N_CTX = 8


def layout_plan(key):
    base_key = jax.random.fold_in(key, 7101)
    half_count = N_CTX // 2
    per_device = TOKENS_PER_SHARD // PIECE
    per_slot = SLOTS // PIECE
    owner_cycle = jax.random.permutation(jax.random.fold_in(base_key, 1), N_CTX).astype(jnp.int32)
    sources = jnp.arange(N_CTX, dtype=jnp.int32)
    chosen = owner_cycle[(sources[:, None] + jnp.arange(half_count, dtype=jnp.int32)[None, :]) % N_CTX]
    listed = jnp.repeat(chosen, per_slot, axis=1)
    shuffle_keys = jax.random.split(jax.random.fold_in(base_key, 2), N_CTX)
    shuffled = jax.vmap(lambda subkey, listing: jax.random.permutation(subkey, listing))(shuffle_keys, listed)
    owner_flat = shuffled.reshape(-1).astype(jnp.int32)
    onehot = (owner_flat[:, None] == jnp.arange(N_CTX, dtype=jnp.int32)[None, :]).astype(jnp.int32)
    arrival = jnp.sum((jnp.cumsum(onehot, axis=0) - 1) * onehot, axis=1)
    cut_keys = jax.random.split(jax.random.fold_in(base_key, 3), N_CTX)

    def cuts_for(subkey):
        return jax.random.permutation(subkey, per_device - 1)[:DOCS_OWN - 1].astype(jnp.int32) + 1
    cut_points = jax.vmap(cuts_for)(cut_keys)
    cut_points = cut_points.at[0].set(jnp.arange(1, DOCS_OWN, dtype=jnp.int32))
    owner_cuts = cut_points[owner_flat]
    passed = owner_cuts <= arrival[:, None]
    doc_local = jnp.sum(passed.astype(jnp.int32), axis=1)
    doc_start = jnp.max(jnp.where(passed, owner_cuts, 0), axis=1)
    offsets = ((arrival - doc_start) * PIECE).astype(jnp.int32)
    labels = jax.random.permutation(jax.random.fold_in(base_key, 4), NDOC).astype(jnp.int32)
    piece_docs = labels[owner_flat * DOCS_OWN + doc_local]
    owners_of = jnp.arange(NDOC, dtype=jnp.int32) // DOCS_OWN
    owner_table = jnp.zeros((NDOC,), jnp.int32).at[labels].set(owners_of)
    return (piece_docs, offsets, owner_table)


def draw_piece_doc(key, part):
    return layout_plan(key)[0]


def draw_piece_offset(key, part):
    return layout_plan(key)[1]


def draw_doc_owner(key, part):
    return layout_plan(key)[2]


def draw_normed_input(key, part):
    normal_base = jnp.clip(jax.random.normal(jax.random.fold_in(key, 11), (TOKENS, MODEL_WIDTH), jnp.float32), -6.0, 6.0)
    return normal_base.astype(jnp.bfloat16)


def shard_levels(rng, extent, shards, low, largest):
    level, own = 1.0, jax.random.fold_in(rng, 6)
    for dim, shards_of in shards:
        steps = jnp.exp(jax.random.uniform(jax.random.fold_in(own, dim), (shards_of,), jnp.float32, low / len(shards), largest / len(shards)))
        level = level * jnp.repeat(steps, extent[dim] // shards_of).reshape([-1 if axis == dim else 1 for axis in range(len(extent))])
    return level


def normal_values(stream_key, dims, scale, limit, shards=(), held_as=jnp.bfloat16):
    array = jax.random.normal(stream_key, dims, jnp.float32) * scale
    if len(shards) > 0:
        array = shard_levels(stream_key, dims, shards, -0.22, 0.18) * array
    return jnp.clip(array, min=-limit, max=limit).astype(held_as)


def setup_inputs(seed: int = 0) -> dict:
    splits = jax.random.split(jax.random.key(seed), 10)
    normed_input = draw_normed_input(jax.random.fold_in(splits[9], 71), 0)
    w_query = normal_values(splits[1], (MODEL_WIDTH, QUERY_HEAD_COUNT * HEAD_SIZE), MODEL_WIDTH ** -0.5, 0.09375, ((1, 4),))
    key_weight = normal_values(splits[2], (MODEL_WIDTH, KV_HEAD_COUNT * HEAD_SIZE), MODEL_WIDTH ** -0.5, 0.09375, ((1, 4),))
    value_weight = normal_values(splits[3], (MODEL_WIDTH, KV_HEAD_COUNT * HEAD_SIZE), MODEL_WIDTH ** -0.5, 0.09375, ((1, 4),))
    output_weight = normal_values(splits[4], (MODEL_WIDTH, QUERY_HEAD_COUNT * HEAD_SIZE), (QUERY_HEAD_COUNT * HEAD_SIZE) ** -0.5, 0.125, ((1, 4),))
    output_cotangent = normal_values(splits[5], (TOKENS, MODEL_WIDTH), 1.0, 6.0, ((0, 8),))
    piece_doc = draw_piece_doc(jax.random.fold_in(splits[9], 71), 0)
    piece_offset = draw_piece_offset(jax.random.fold_in(splits[9], 71), 0)
    doc_owner = draw_doc_owner(jax.random.fold_in(splits[9], 71), 0)
    return {"normed_input": normed_input, "w_query": w_query, "key_weight": key_weight, "value_weight": value_weight, "output_weight": output_weight, "output_cotangent": output_cotangent, "piece_doc": piece_doc, "piece_offset": piece_offset, "doc_owner": doc_owner}


rope_base = 500000.0
fill_value = -1e+30

def apply_rotary(heads, positions, direction):
    half_width = heads.shape[-1] // 2
    frequency = rope_base ** (-2.0 * jnp.arange(half_width, dtype=jnp.float32) / heads.shape[-1])
    angles = positions.astype(jnp.float32)[:, None] * frequency[None, :]
    cosine = jnp.cos(angles)[:, None, :]
    sine_term = direction * jnp.sin(angles)[:, None, :]
    lower_half = heads[..., :half_width]
    upper_half = heads[..., half_width:]
    return jnp.concatenate([lower_half * cosine - upper_half * sine_term, upper_half * cosine + lower_half * sine_term], axis=-1)

def mask_of(query_doc, query_pos, query_live, key_doc, key_pos, key_live):
    return (query_doc[:, None] == key_doc[None, :]) & (key_pos[None, :] <= query_pos[:, None]) & query_live[:, None] & key_live[None, :]

def attend_scores(query_matrix, key_heads, score_scale):
    return jnp.einsum('bkgd,mkd->kgbm', query_matrix.astype(jnp.float32), key_heads.astype(jnp.float32)) * score_scale

def attend_forward(query_matrix, key_heads, value_heads, allowed, score_scale):
    scores = attend_scores(query_matrix, key_heads, score_scale)
    row_max = lax.optimization_barrier(jnp.max(jnp.where(allowed, scores, fill_value), axis=-1))
    exponent = jnp.where(allowed, jnp.exp(scores - row_max[..., None]), 0.0)
    row_sum = lax.optimization_barrier(jnp.sum(exponent, axis=-1))
    row_sum = jnp.where(jnp.any(allowed, axis=-1), row_sum, 1.0)
    probability = (exponent / row_sum[..., None]).astype(jnp.bfloat16)
    attended_output = jnp.einsum('kgbm,mkd->bkgd', probability.astype(jnp.float32), value_heads.astype(jnp.float32))
    return (attended_output.astype(jnp.bfloat16), row_max, row_sum)

def attend_backward(query_matrix, key_heads, value_heads, out_grads, attended_output, row_max, row_sum, allowed, score_scale):
    scores = attend_scores(query_matrix, key_heads, score_scale)
    probability = jnp.where(allowed, jnp.exp(scores - row_max[..., None]), 0.0) / row_sum[..., None]
    rounded = probability.astype(jnp.bfloat16)
    row_delta = jnp.einsum('bkgd,bkgd->kgb', out_grads.astype(jnp.float32), attended_output.astype(jnp.float32))
    prob_grad = jnp.einsum('bkgd,mkd->kgbm', out_grads.astype(jnp.float32), value_heads.astype(jnp.float32))
    score_grad = (probability * (prob_grad - row_delta[..., None])).astype(jnp.bfloat16)
    query_gradient = jnp.einsum('kgbm,mkd->bkgd', score_grad.astype(jnp.float32), key_heads.astype(jnp.float32)) * score_scale
    key_gradient = jnp.einsum('kgbm,bkgd->mkd', score_grad.astype(jnp.float32), query_matrix.astype(jnp.float32)) * score_scale
    value_gradient = jnp.einsum('kgbm,bkgd->mkd', rounded.astype(jnp.float32), out_grads.astype(jnp.float32))
    return (query_gradient, key_gradient, value_gradient)

def reference(normed_input, w_query, key_weight, value_weight, output_weight, output_cotangent, piece_doc, piece_offset, doc_owner):
    token_list = normed_input.shape[0]
    group_width = QUERY_HEAD_COUNT // KV_HEAD_COUNT
    score_scale = 1.0 / math.sqrt(HEAD_SIZE)
    within = jnp.arange(PIECE, dtype=jnp.int32)
    token_doc = jnp.repeat(piece_doc, PIECE)
    token_position = (piece_offset[:, None] + within[None, :]).reshape(-1)
    token_owner = doc_owner[token_doc]
    owner_order = jnp.argsort(token_owner, stable=True).astype(jnp.int32).reshape(N_CTX, TOKENS_PER_SHARD)
    query_row_block = apply_rotary(jnp.dot(normed_input, w_query, preferred_element_type=jnp.float32).reshape(token_list, QUERY_HEAD_COUNT, HEAD_SIZE), token_position, 1.0).astype(jnp.bfloat16)
    key_row_block = apply_rotary(jnp.dot(normed_input, key_weight, preferred_element_type=jnp.float32).reshape(token_list, KV_HEAD_COUNT, HEAD_SIZE), token_position, 1.0).astype(jnp.bfloat16)
    value_row_block = jnp.dot(normed_input, value_weight, preferred_element_type=jnp.float32).astype(jnp.bfloat16).reshape(token_list, KV_HEAD_COUNT, HEAD_SIZE)
    head_gradient = jnp.dot(output_cotangent, output_weight, preferred_element_type=jnp.float32).astype(jnp.bfloat16).reshape(token_list, KV_HEAD_COUNT, group_width, HEAD_SIZE)

    def per_owner(group_members):
        query_matrix = query_row_block[group_members].reshape(TOKENS_PER_SHARD, KV_HEAD_COUNT, group_width, HEAD_SIZE)
        key_heads = key_row_block[group_members]
        value_heads = value_row_block[group_members]
        out_grads = head_gradient[group_members]
        docs = token_doc[group_members]
        positions = token_position[group_members]
        live_rows = jnp.ones((TOKENS_PER_SHARD,), dtype=bool)
        allowed = mask_of(docs, positions, live_rows, docs, positions, live_rows)
        attended_output, row_max, row_sum = attend_forward(query_matrix, key_heads, value_heads, allowed, score_scale)
        query_gradient, key_gradient, value_gradient = attend_backward(query_matrix, key_heads, value_heads, out_grads, attended_output, row_max, row_sum, allowed, score_scale)
        query_gradient = apply_rotary(query_gradient.reshape(TOKENS_PER_SHARD, QUERY_HEAD_COUNT, HEAD_SIZE), positions, -1.0).astype(jnp.bfloat16)
        key_gradient = apply_rotary(key_gradient, positions, -1.0).astype(jnp.bfloat16)
        return (attended_output.reshape(TOKENS_PER_SHARD, QUERY_HEAD_COUNT * HEAD_SIZE), query_gradient.reshape(TOKENS_PER_SHARD, QUERY_HEAD_COUNT * HEAD_SIZE), key_gradient.reshape(TOKENS_PER_SHARD, KV_HEAD_COUNT * HEAD_SIZE), value_gradient.astype(jnp.bfloat16).reshape(TOKENS_PER_SHARD, KV_HEAD_COUNT * HEAD_SIZE))
    outputs = lax.map(per_owner, owner_order)
    flat_order = owner_order.reshape(-1)

    def place(stacked):
        return jnp.zeros((token_list, stacked.shape[-1]), stacked.dtype).at[flat_order].set(stacked.reshape(token_list, -1))
    attended_output = place(outputs[0])
    query_gradient = place(outputs[1])
    key_gradient = place(outputs[2])
    value_gradient = place(outputs[3])
    grad_in = (jnp.dot(query_gradient, w_query.T, preferred_element_type=jnp.float32) + jnp.dot(key_gradient, key_weight.T, preferred_element_type=jnp.float32) + jnp.dot(value_gradient, value_weight.T, preferred_element_type=jnp.float32)).astype(jnp.bfloat16)
    grad_query = jnp.dot(normed_input.T, query_gradient, preferred_element_type=jnp.float32).astype(jnp.bfloat16)
    grad_key = jnp.dot(normed_input.T, key_gradient, preferred_element_type=jnp.float32).astype(jnp.bfloat16)
    grad_value = jnp.dot(normed_input.T, value_gradient, preferred_element_type=jnp.float32).astype(jnp.bfloat16)
    grad_out = jnp.dot(output_cotangent.T, attended_output, preferred_element_type=jnp.float32).astype(jnp.bfloat16)
    return (grad_in, grad_query, grad_key, grad_value, grad_out)
```

```python
import math

import jax
import jax.numpy as jnp
from jax import lax
from jax.sharding import PartitionSpec as P

HEAD_SIZE = 128
PIECE = 8


rope_base = 500000.0
fill_value = -1e30


def apply_rotary(heads, positions, direction):
    half_width = heads.shape[-1] // 2
    frequency = rope_base ** (-2.0 * jnp.arange(half_width, dtype=jnp.float32) / heads.shape[-1])
    angles = positions.astype(jnp.float32)[:, None] * frequency[None, :]
    cosine = jnp.cos(angles)[:, None, :]
    sine_term = direction * jnp.sin(angles)[:, None, :]
    lower_half = heads[..., :half_width]
    upper_half = heads[..., half_width:]
    return jnp.concatenate(
        [
            lower_half * cosine - upper_half * sine_term,
            upper_half * cosine + lower_half * sine_term,
        ],
        axis=-1,
    )


def mask_of(query_doc, query_pos, key_doc, key_pos):
    return (query_doc[:, None] == key_doc[None, :]) & (key_pos[None, :] <= query_pos[:, None])


def attend_both(query_matrix, key_heads, value_heads, out_grads, allowed, score_scale):
    scores = (
        jnp.einsum("bkgd,mkd->kgbm", query_matrix, key_heads, preferred_element_type=jnp.float32)
        * score_scale
    )
    scores = jnp.where(allowed, scores, fill_value)
    row_max = jnp.max(scores, axis=-1, keepdims=True)
    exponent = jnp.where(allowed, jnp.exp(scores - row_max), 0.0)
    row_sum = jnp.sum(exponent, axis=-1, keepdims=True)
    probability = exponent / row_sum
    rounded = probability.astype(jnp.bfloat16)
    attended = jnp.einsum(
        "kgbm,mkd->bkgd", rounded, value_heads, preferred_element_type=jnp.float32
    ).astype(jnp.bfloat16)
    row_delta = jnp.einsum(
        "bkgd,bkgd->kgb", out_grads.astype(jnp.float32), attended.astype(jnp.float32)
    )
    prob_grad = jnp.einsum(
        "bkgd,mkd->kgbm", out_grads, value_heads, preferred_element_type=jnp.float32
    )
    score_grad = (probability * (prob_grad - row_delta[..., None])).astype(jnp.bfloat16)
    query_gradient = (
        jnp.einsum("kgbm,mkd->bkgd", score_grad, key_heads, preferred_element_type=jnp.float32)
        * score_scale
    )
    key_gradient = (
        jnp.einsum("kgbm,bkgd->mkd", score_grad, query_matrix, preferred_element_type=jnp.float32)
        * score_scale
    )
    value_gradient = jnp.einsum(
        "kgbm,bkgd->mkd", rounded, out_grads, preferred_element_type=jnp.float32
    )
    return attended, query_gradient, key_gradient, value_gradient


def contract_rows(left, right):
    return lax.dot_general(
        left, right, (((0,), (0,)), ((), ())), preferred_element_type=jnp.float32
    )


def contract_cols(left, right):
    return lax.dot_general(
        left, right, (((1,), (1,)), ((), ())), preferred_element_type=jnp.float32
    )


def ring_order(count):
    if count % 2:
        return list(range(count))
    return list(range(0, count, 2)) + list(range(count - 1, 0, -2))


def ring_steps(product, axis, step):
    count = lax.axis_size(axis)
    order = ring_order(count)
    place = [0] * count
    for spot, device in enumerate(order):
        place[device] = spot
    here = jnp.asarray(place, jnp.int32)[lax.axis_index(axis)]
    order_table = jnp.asarray(order, jnp.int32)
    pairs = [(order[i], order[(i + step) % count]) for i in range(count)]
    total = None
    for hop in range(count):
        block = order_table[(here - step * (1 + hop)) % count]
        term = product(block)
        if hop > 0:
            term = term + lax.ppermute(total, axis, pairs).astype(jnp.float32)
        total = term.astype(jnp.bfloat16)
        yield total


def run_rings(rings):
    results = [None] * len(rings)
    for totals in zip(*rings):
        results = list(totals)
    return results


def halving_sum(blocks, axis):
    count = len(blocks)
    index = lax.axis_index(axis)
    bit = 1
    while len(blocks) > 1:
        upper = (index & bit) != 0
        pairs = [(i, i ^ bit) for i in range(count)]
        sums = []
        for low, high in zip(blocks[0::2], blocks[1::2]):
            sent = jnp.where(upper, low, high).astype(jnp.bfloat16)
            kept = jnp.where(upper, high, low)
            sums.append(kept + lax.ppermute(sent, axis, pairs).astype(jnp.float32))
        blocks = sums
        bit *= 2
    return blocks[0]


def on_device(
    normed_input,
    w_query,
    key_weight,
    value_weight,
    output_weight,
    output_cotangent,
    piece_doc,
    piece_offset,
    doc_owner,
):
    sources = lax.axis_size("ctx")
    splits = lax.axis_size("tp")
    self_index = lax.axis_index("ctx")
    tok_rows, model_width = normed_input.shape
    local_q = w_query.shape[1] // HEAD_SIZE
    local_kv = key_weight.shape[1] // HEAD_SIZE
    group_width = local_q // local_kv
    q_width = w_query.shape[1]
    kv_width = key_weight.shape[1]
    per_device = tok_rows // PIECE
    slot_rows = 2 * tok_rows // sources
    per_slot = slot_rows // PIECE
    owner_rows = sources * slot_rows
    score_scale = 1.0 / math.sqrt(HEAD_SIZE)
    within = jnp.arange(PIECE, dtype=jnp.int32)
    slot_ids = jnp.arange(per_slot, dtype=jnp.int32)
    doc_ids = jnp.arange(doc_owner.shape[0], dtype=jnp.int32)
    piece_owner = jnp.sum(
        jnp.where(piece_doc[:, None] == doc_ids[None, :], doc_owner[None, :], 0), axis=1
    )
    own_owner = lax.dynamic_slice_in_dim(piece_owner, self_index * per_device, per_device)
    own_offset = lax.dynamic_slice_in_dim(piece_offset, self_index * per_device, per_device)
    own_pos = (own_offset[:, None] + within[None, :]).reshape(-1)
    piece_ids = jnp.arange(per_device, dtype=jnp.int32)
    earlier = (own_owner[:, None] == own_owner[None, :]) & (piece_ids[None, :] < piece_ids[:, None])
    own_rank = jnp.sum(earlier.astype(jnp.int32), axis=1)
    own_slot = own_owner * per_slot + own_rank
    own_row = (own_slot[:, None] * PIECE + within[None, :]).reshape(-1)
    placing = (jnp.arange(owner_rows, dtype=jnp.int32)[:, None] == own_row[None, :]).astype(
        jnp.bfloat16
    )

    def to_slots(matrix):
        return jnp.dot(placing, matrix, preferred_element_type=jnp.float32).astype(jnp.bfloat16)

    def from_slots(matrix):
        return contract_rows(placing, matrix).astype(jnp.bfloat16)

    def exchange(matrix):
        return lax.all_to_all(matrix, "ctx", split_axis=0, concat_axis=0, tiled=True)

    grad_rows = jnp.dot(output_cotangent, output_weight, preferred_element_type=jnp.float32).astype(
        jnp.bfloat16
    )
    got_grad = exchange(to_slots(grad_rows))
    query_rows = apply_rotary(
        jnp.dot(normed_input, w_query, preferred_element_type=jnp.float32).reshape(
            tok_rows, local_q, HEAD_SIZE
        ),
        own_pos,
        1.0,
    )
    query_rows = query_rows.astype(jnp.bfloat16).reshape(tok_rows, q_width)
    got_query = exchange(to_slots(query_rows))
    pair_rows = jnp.dot(
        normed_input,
        jnp.concatenate([key_weight, value_weight], axis=1),
        preferred_element_type=jnp.float32,
    )
    key_rows = apply_rotary(
        pair_rows[:, :kv_width].reshape(tok_rows, local_kv, HEAD_SIZE), own_pos, 1.0
    )
    key_rows = key_rows.reshape(tok_rows, kv_width)
    pair_rows = jnp.concatenate([key_rows, pair_rows[:, kv_width:]], axis=1).astype(jnp.bfloat16)
    got_pair = exchange(to_slots(pair_rows))

    owner_grid = piece_owner.reshape(sources, per_device)
    doc_grid = piece_doc.reshape(sources, per_device)
    offset_grid = piece_offset.reshape(sources, per_device)
    mine_hits = (owner_grid == self_index).astype(jnp.int32)
    mine_rank = jnp.cumsum(mine_hits, axis=1) - 1
    picked = (mine_hits[:, None, :] == 1) & (mine_rank[:, None, :] == slot_ids[None, :, None])
    slot_doc = jnp.sum(jnp.where(picked, doc_grid[:, None, :], 0), axis=2).reshape(-1)
    slot_offset = jnp.sum(jnp.where(picked, offset_grid[:, None, :], 0), axis=2).reshape(-1)
    slot_live = jnp.any(picked, axis=2).reshape(-1)
    live_rank = jnp.cumsum(slot_live.astype(jnp.int32)) - 1
    choosing = slot_live[None, :] & (live_rank[None, :] == piece_ids[:, None])
    compact_doc = jnp.sum(jnp.where(choosing, slot_doc[None, :], 0), axis=1)
    compact_offset = jnp.sum(jnp.where(choosing, slot_offset[None, :], 0), axis=1)
    slot_row = jnp.where(slot_live, live_rank * PIECE, -PIECE)
    slot_row = (slot_row[:, None] + within[None, :]).reshape(-1)
    packing = (jnp.arange(tok_rows, dtype=jnp.int32)[:, None] == slot_row[None, :]).astype(
        jnp.bfloat16
    )

    def to_live(matrix):
        return jnp.dot(packing, matrix, preferred_element_type=jnp.float32).astype(jnp.bfloat16)

    def to_owner_slots(matrix):
        return contract_rows(packing, matrix).astype(jnp.bfloat16)

    row_doc = jnp.repeat(compact_doc, PIECE)
    row_pos = (compact_offset[:, None] + within[None, :]).reshape(-1)
    live_pair = to_live(got_pair)
    attended, query_gradient, key_gradient, value_gradient = attend_both(
        to_live(got_query).reshape(tok_rows, local_kv, group_width, HEAD_SIZE),
        live_pair[:, :kv_width].reshape(tok_rows, local_kv, HEAD_SIZE),
        live_pair[:, kv_width:].reshape(tok_rows, local_kv, HEAD_SIZE),
        to_live(got_grad).reshape(tok_rows, local_kv, group_width, HEAD_SIZE),
        mask_of(row_doc, row_pos, row_doc, row_pos),
        score_scale,
    )
    back_attended = exchange(to_owner_slots(attended.reshape(tok_rows, q_width)))
    query_gradient = apply_rotary(
        query_gradient.reshape(tok_rows, local_q, HEAD_SIZE), row_pos, -1.0
    )
    key_gradient = apply_rotary(key_gradient, row_pos, -1.0)
    gradients = jnp.concatenate(
        [
            query_gradient.reshape(tok_rows, q_width),
            key_gradient.reshape(tok_rows, kv_width),
            value_gradient.reshape(tok_rows, kv_width),
        ],
        axis=1,
    ).astype(jnp.bfloat16)
    back_gradients = exchange(to_owner_slots(gradients))
    local_attended = from_slots(back_attended)
    local_gradients = from_slots(back_gradients)

    block_width = model_width // sources

    def product_of(left, right):
        def product(block):
            rows = lax.dynamic_slice_in_dim(left, block * block_width, block_width, axis=1)
            return contract_rows(rows, right)

        return product

    half_grad = local_gradients.shape[1] // 2
    half_out = q_width // 2
    grad_low, out_low, grad_high, out_high = run_rings(
        [
            ring_steps(product_of(normed_input, local_gradients[:, :half_grad]), "ctx", 1),
            ring_steps(product_of(output_cotangent, local_attended[:, :half_out]), "ctx", 1),
            ring_steps(product_of(normed_input, local_gradients[:, half_grad:]), "ctx", -1),
            ring_steps(product_of(output_cotangent, local_attended[:, half_out:]), "ctx", -1),
        ]
    )
    grads = jnp.concatenate([grad_low, grad_high], axis=1)
    grad_query = grads[:, :q_width]
    grad_key = grads[:, q_width : q_width + kv_width]
    grad_value = grads[:, q_width + kv_width :]
    grad_out = jnp.concatenate([out_low, out_high], axis=1)

    input_term = (
        contract_cols(local_gradients[:, :q_width], w_query)
        + contract_cols(local_gradients[:, q_width : q_width + kv_width], key_weight)
        + contract_cols(local_gradients[:, q_width + kv_width :], value_weight)
    )
    if splits & (splits - 1) == 0:
        grad_in = halving_sum(jnp.split(input_term, splits, axis=1), "tp")
    else:
        grad_in = lax.psum_scatter(input_term, "tp", scatter_dimension=1, tiled=True)
    return (grad_in.astype(jnp.bfloat16), grad_query, grad_key, grad_value, grad_out)


def solution(mesh):
    return jax.shard_map(
        on_device,
        mesh=mesh,
        in_specs=(
            P("ctx", None),
            P(None, "tp"),
            P(None, "tp"),
            P(None, "tp"),
            P(None, "tp"),
            P("ctx", None),
            P(),
            P(),
            P(),
        ),
        out_specs=(P("ctx", "tp"), P("ctx", "tp"), P("ctx", "tp"), P("ctx", "tp"), P("ctx", "tp")),
        check_vma=False,
    )
```

```python
import functools
import math

import jax
import jax.numpy as jnp
from jax import lax
from jax.experimental import pallas as pl
from jax.experimental.pallas import tpu as pltpu
from jax.sharding import PartitionSpec as P

HEAD_SIZE = 128
PIECE = 8


rope_base = 500000.0
fill_value = -1e30


def apply_rotary(heads, positions, direction):
    half_width = heads.shape[-1] // 2
    frequency = rope_base ** (-2.0 * jnp.arange(half_width, dtype=jnp.float32) / heads.shape[-1])
    angles = positions.astype(jnp.float32)[:, None] * frequency[None, :]
    cosine = jnp.cos(angles)[:, None, :]
    sine_term = direction * jnp.sin(angles)[:, None, :]
    lower_half = heads[..., :half_width]
    upper_half = heads[..., half_width:]
    return jnp.concatenate(
        [
            lower_half * cosine - upper_half * sine_term,
            upper_half * cosine + lower_half * sine_term,
        ],
        axis=-1,
    )


def mask_of(query_doc, query_pos, key_doc, key_pos):
    return (query_doc[:, None] == key_doc[None, :]) & (key_pos[None, :] <= query_pos[:, None])


def attend_both(query_matrix, key_heads, value_heads, out_grads, allowed, score_scale):
    scores = (
        jnp.einsum("bkgd,mkd->kgbm", query_matrix, key_heads, preferred_element_type=jnp.float32)
        * score_scale
    )
    scores = jnp.where(allowed, scores, fill_value)
    row_max = jnp.max(scores, axis=-1, keepdims=True)
    exponent = jnp.where(allowed, jnp.exp(scores - row_max), 0.0)
    row_sum = jnp.sum(exponent, axis=-1, keepdims=True)
    probability = exponent / row_sum
    rounded = probability.astype(jnp.bfloat16)
    attended = jnp.einsum(
        "kgbm,mkd->bkgd", rounded, value_heads, preferred_element_type=jnp.float32
    ).astype(jnp.bfloat16)
    row_delta = jnp.einsum(
        "bkgd,bkgd->kgb", out_grads.astype(jnp.float32), attended.astype(jnp.float32)
    )
    prob_grad = jnp.einsum(
        "bkgd,mkd->kgbm", out_grads, value_heads, preferred_element_type=jnp.float32
    )
    score_grad = (probability * (prob_grad - row_delta[..., None])).astype(jnp.bfloat16)
    query_gradient = (
        jnp.einsum("kgbm,mkd->bkgd", score_grad, key_heads, preferred_element_type=jnp.float32)
        * score_scale
    )
    key_gradient = (
        jnp.einsum("kgbm,bkgd->mkd", score_grad, query_matrix, preferred_element_type=jnp.float32)
        * score_scale
    )
    value_gradient = jnp.einsum(
        "kgbm,bkgd->mkd", rounded, out_grads, preferred_element_type=jnp.float32
    )
    return attended, query_gradient, key_gradient, value_gradient


def contract_rows(left, right):
    return lax.dot_general(
        left, right, (((0,), (0,)), ((), ())), preferred_element_type=jnp.float32
    )


def contract_cols(left, right):
    return lax.dot_general(
        left, right, (((1,), (1,)), ((), ())), preferred_element_type=jnp.float32
    )


def spot_of(device, count):
    odd = lax.rem(device, 2)
    half = lax.div(device, 2)
    return (1 - odd) * half + odd * (count - 1 - half)


def device_at(spot, count):
    high = lax.div(spot, count // 2)
    return (1 - high) * (2 * spot) + high * (2 * (count - 1 - spot) + 1)


def sums_kernel(
    count,
    q_width,
    kv_width,
    input_t,
    cotangent_t,
    weights,
    gradients,
    attended,
    grad_in,
    grad_query,
    grad_key,
    grad_value,
    grad_out,
    ring0,
    ring1,
    ring2,
    ring3,
    near_sent,
    near_got,
    far_sent,
    far_got,
    ring_send,
    ring_recv,
    tp_send,
    tp_recv,
):
    me = lax.axis_index("ctx")
    tp = lax.axis_index("tp")
    here = spot_of(me, count)
    after = device_at(lax.rem(here + 1, count), count)
    before = device_at(lax.rem(here + count - 1, count), count)
    low_bit = lax.rem(tp, 2)
    high_bit = lax.div(tp, 2)
    near = tp + 1 - 2 * low_bit
    far = tp + 2 - 4 * high_bit
    mesh_id = pl.DeviceIdType.MESH
    barrier = pltpu.get_barrier_semaphore()
    for target in ((after, tp), (before, tp), (me, near), (me, far)):
        pl.semaphore_signal(barrier, inc=1, device_id=target, device_id_type=mesh_id)
    pl.semaphore_wait(barrier, 4)

    block_rows = input_t.shape[0] // count
    half_grad = gradients.shape[1] // 2
    half_out = attended.shape[1] // 2
    rings = (
        (ring0, input_t, gradients, 0, half_grad, 1),
        (ring1, input_t, gradients, half_grad, half_grad, -1),
        (ring2, cotangent_t, attended, 0, half_out, 1),
        (ring3, cotangent_t, attended, half_out, half_out, -1),
    )

    def term(ring, hop):
        _, left, right, start, width, step = rings[ring]
        if step > 0:
            spot = lax.rem(here + 2 * count - 1 - hop, count)
        else:
            spot = lax.rem(here + 1 + hop, count)
        row = pl.multiple_of(device_at(spot, count) * block_rows, block_rows)
        return jnp.dot(
            left[pl.ds(row, block_rows), :],
            right[:, start : start + width],
            preferred_element_type=jnp.float32,
        )

    def ring_copy(ring, hop):
        buffer = rings[ring][0]
        return pltpu.make_async_remote_copy(
            src_ref=buffer.at[hop],
            dst_ref=buffer.at[hop + 1],
            send_sem=ring_send.at[ring, hop],
            recv_sem=ring_recv.at[ring, hop],
            device_id=(after if rings[ring][5] > 0 else before, tp),
            device_id_type=mesh_id,
        )

    for ring in range(4):
        rings[ring][0][0] = term(ring, 0).astype(jnp.bfloat16)
        ring_copy(ring, 0).start()

    def input_term(chunk):
        rows = grad_in.shape[1]
        row = pl.multiple_of(chunk * rows, rows)
        return lax.dot_general(
            gradients[...],
            weights[pl.ds(row, rows), :],
            (((1,), (1,)), ((), ())),
            preferred_element_type=jnp.float32,
        )

    def near_copy(slot):
        return pltpu.make_async_remote_copy(
            src_ref=near_sent.at[slot],
            dst_ref=near_got.at[slot],
            send_sem=tp_send.at[slot],
            recv_sem=tp_recv.at[slot],
            device_id=(me, near),
            device_id_type=mesh_id,
        )

    far_copy = pltpu.make_async_remote_copy(
        src_ref=far_sent,
        dst_ref=far_got,
        send_sem=tp_send.at[2],
        recv_sem=tp_recv.at[2],
        device_id=(me, far),
        device_id_type=mesh_id,
    )

    near_sent[0] = input_term(2 * (1 - high_bit) + 1 - low_bit).astype(jnp.bfloat16)
    near_copy(0).start()
    near_sent[1] = input_term(2 * high_bit + 1 - low_bit).astype(jnp.bfloat16)
    near_copy(1).start()

    def ring_hop(hop, carry):
        for ring in range(4):
            ring_copy(ring, hop - 1).wait_recv()
            buffer = rings[ring][0]
            total = term(ring, hop) + buffer[hop].astype(jnp.float32)
            buffer[hop] = total.astype(jnp.bfloat16)
            ring_copy(ring, hop).start()
        return carry

    early = min(2, count - 1)
    lax.fori_loop(1, early, ring_hop, 0)
    near_copy(0).wait_recv()
    far_sent[...] = (
        input_term(2 * (1 - high_bit) + low_bit) + near_got[0].astype(jnp.float32)
    ).astype(jnp.bfloat16)
    far_copy.start()
    lax.fori_loop(early, count - 1, ring_hop, 0)

    near_copy(1).wait_recv()
    far_copy.wait_recv()
    grad_in[...] = (
        input_term(2 * high_bit + low_bit)
        + near_got[1].astype(jnp.float32)
        + far_got[...].astype(jnp.float32)
    ).astype(jnp.bfloat16)

    pieces = (
        (grad_query, 0, q_width),
        (grad_key, q_width, kv_width),
        (grad_value, q_width + kv_width, kv_width),
    )
    for ring in range(4):
        ring_copy(ring, count - 2).wait_recv()
        buffer, _, right, start, width, _ = rings[ring]
        total = term(ring, count - 1) + buffer[count - 1].astype(jnp.float32)
        total = total.astype(jnp.bfloat16)
        if right is attended:
            grad_out[:, start : start + width] = total
        else:
            for target, low, size in pieces:
                first, last = max(low, start), min(low + size, start + width)
                if first < last:
                    target[:, first - low : last - low] = total[:, first - start : last - start]

    def drain(hop, carry):
        for ring in range(4):
            ring_copy(ring, hop).wait_send()
        return carry

    lax.fori_loop(0, count - 1, drain, 0)
    near_copy(0).wait_send()
    near_copy(1).wait_send()
    far_copy.wait_send()


def sum_products(input_t, cotangent_t, weights, gradients, attended, count, q_width, kv_width):
    model_width, tok_rows = input_t.shape
    block_rows = model_width // count
    in_width = model_width // 4
    half_grad = gradients.shape[1] // 2
    half_out = attended.shape[1] // 2
    half = jnp.bfloat16
    flops = 2 * tok_rows * model_width * (2 * gradients.shape[1] + attended.shape[1])
    vmem = pl.BlockSpec(memory_space=pltpu.VMEM)
    return pl.pallas_call(
        functools.partial(sums_kernel, count, q_width, kv_width),
        out_shape=(
            jax.ShapeDtypeStruct((tok_rows, in_width), half),
            jax.ShapeDtypeStruct((block_rows, q_width), half),
            jax.ShapeDtypeStruct((block_rows, kv_width), half),
            jax.ShapeDtypeStruct((block_rows, kv_width), half),
            jax.ShapeDtypeStruct((block_rows, q_width), half),
        ),
        in_specs=[vmem] * 5,
        out_specs=(vmem,) * 5,
        scratch_shapes=[
            pltpu.VMEM((count, block_rows, half_grad), half),
            pltpu.VMEM((count, block_rows, half_grad), half),
            pltpu.VMEM((count, block_rows, half_out), half),
            pltpu.VMEM((count, block_rows, half_out), half),
            pltpu.VMEM((2, tok_rows, in_width), half),
            pltpu.VMEM((2, tok_rows, in_width), half),
            pltpu.VMEM((tok_rows, in_width), half),
            pltpu.VMEM((tok_rows, in_width), half),
            pltpu.SemaphoreType.DMA((4, count - 1)),
            pltpu.SemaphoreType.DMA((4, count - 1)),
            pltpu.SemaphoreType.DMA((3,)),
            pltpu.SemaphoreType.DMA((3,)),
        ],
        compiler_params=pltpu.CompilerParams(
            collective_id=0, has_side_effects=True, vmem_limit_bytes=56 * 1024 * 1024
        ),
        cost_estimate=pl.CostEstimate(
            flops=flops, bytes_accessed=30 * model_width * tok_rows, transcendentals=0
        ),
    )(input_t, cotangent_t, weights, gradients, attended)


def on_device(
    normed_input,
    w_query,
    key_weight,
    value_weight,
    output_weight,
    output_cotangent,
    piece_doc,
    piece_offset,
    doc_owner,
):
    sources = lax.axis_size("ctx")
    self_index = lax.axis_index("ctx")
    tok_rows = normed_input.shape[0]
    local_q = w_query.shape[1] // HEAD_SIZE
    local_kv = key_weight.shape[1] // HEAD_SIZE
    group_width = local_q // local_kv
    q_width = w_query.shape[1]
    kv_width = key_weight.shape[1]
    per_device = tok_rows // PIECE
    slot_rows = 2 * tok_rows // sources
    per_slot = slot_rows // PIECE
    owner_rows = sources * slot_rows
    score_scale = 1.0 / math.sqrt(HEAD_SIZE)
    within = jnp.arange(PIECE, dtype=jnp.int32)
    doc_ids = jnp.arange(doc_owner.shape[0], dtype=jnp.int32)
    piece_owner = jnp.sum(
        jnp.where(piece_doc[:, None] == doc_ids[None, :], doc_owner[None, :], 0), axis=1
    )
    own_owner = lax.dynamic_slice_in_dim(piece_owner, self_index * per_device, per_device)
    own_offset = lax.dynamic_slice_in_dim(piece_offset, self_index * per_device, per_device)
    own_pos = (own_offset[:, None] + within[None, :]).reshape(-1)
    piece_ids = jnp.arange(per_device, dtype=jnp.int32)
    earlier = (own_owner[:, None] == own_owner[None, :]) & (piece_ids[None, :] < piece_ids[:, None])
    own_rank = jnp.sum(earlier.astype(jnp.int32), axis=1)
    own_slot = own_owner * per_slot + own_rank
    own_row = (own_slot[:, None] * PIECE + within[None, :]).reshape(-1)
    placing = (jnp.arange(owner_rows, dtype=jnp.int32)[:, None] == own_row[None, :]).astype(
        jnp.bfloat16
    )

    def to_slots(matrix):
        return jnp.dot(placing, matrix, preferred_element_type=jnp.float32).astype(jnp.bfloat16)

    def from_slots(matrix):
        return contract_rows(placing, matrix).astype(jnp.bfloat16)

    def exchange(matrix):
        return lax.all_to_all(matrix, "ctx", split_axis=0, concat_axis=0, tiled=True)

    grad_rows = jnp.dot(output_cotangent, output_weight, preferred_element_type=jnp.float32).astype(
        jnp.bfloat16
    )
    got_grad = exchange(to_slots(grad_rows))
    query_rows = apply_rotary(
        jnp.dot(normed_input, w_query, preferred_element_type=jnp.float32).reshape(
            tok_rows, local_q, HEAD_SIZE
        ),
        own_pos,
        1.0,
    )
    query_rows = query_rows.astype(jnp.bfloat16).reshape(tok_rows, q_width)
    got_query = exchange(to_slots(query_rows))
    all_ids = jnp.arange(piece_owner.shape[0], dtype=jnp.int32)
    mine = piece_owner == self_index
    preceding = mine[None, :] & (all_ids[None, :] < all_ids[:, None])
    same_source = (all_ids[None, :] // per_device) == (all_ids[:, None] // per_device)
    live_rank = jnp.sum(preceding.astype(jnp.int32), axis=1)
    source_rank = jnp.sum((preceding & same_source).astype(jnp.int32), axis=1)
    choosing = mine[None, :] & (live_rank[None, :] == piece_ids[:, None])

    def choose(table):
        return jnp.sum(jnp.where(choosing, table[None, :], 0), axis=1)

    compact_slot = choose(all_ids // per_device * per_slot + source_rank)
    compact_row = (compact_slot[:, None] * PIECE + within[None, :]).reshape(-1)
    packing = (
        jnp.arange(owner_rows, dtype=jnp.int32)[None, :] == compact_row[:, None]
    ).astype(jnp.bfloat16)
    row_doc = jnp.repeat(choose(piece_doc), PIECE)
    row_pos = (choose(piece_offset)[:, None] + within[None, :]).reshape(-1)
    pair_weights = jnp.concatenate([key_weight, value_weight], axis=1)
    weights = jnp.concatenate([w_query, pair_weights], axis=1)
    input_t = normed_input.T
    cotangent_t = output_cotangent.T
    packing, row_doc, row_pos, pair_weights, normed_input = lax.optimization_barrier(
        (packing, row_doc, row_pos, pair_weights, normed_input)
    )
    pair_rows = jnp.dot(normed_input, pair_weights, preferred_element_type=jnp.float32)
    key_rows = apply_rotary(
        pair_rows[:, :kv_width].reshape(tok_rows, local_kv, HEAD_SIZE), own_pos, 1.0
    )
    key_rows = key_rows.reshape(tok_rows, kv_width)
    pair_rows = jnp.concatenate([key_rows, pair_rows[:, kv_width:]], axis=1).astype(jnp.bfloat16)
    got_pair = exchange(to_slots(pair_rows))

    def to_live(matrix):
        return jnp.dot(packing, matrix, preferred_element_type=jnp.float32).astype(jnp.bfloat16)

    def to_owner_slots(matrix):
        return contract_rows(packing, matrix).astype(jnp.bfloat16)

    live_pair = to_live(got_pair)
    attended, query_gradient, key_gradient, value_gradient = attend_both(
        to_live(got_query).reshape(tok_rows, local_kv, group_width, HEAD_SIZE),
        live_pair[:, :kv_width].reshape(tok_rows, local_kv, HEAD_SIZE),
        live_pair[:, kv_width:].reshape(tok_rows, local_kv, HEAD_SIZE),
        to_live(got_grad).reshape(tok_rows, local_kv, group_width, HEAD_SIZE),
        mask_of(row_doc, row_pos, row_doc, row_pos),
        score_scale,
    )
    back_attended = exchange(to_owner_slots(attended.reshape(tok_rows, q_width)))
    query_gradient = apply_rotary(
        query_gradient.reshape(tok_rows, local_q, HEAD_SIZE), row_pos, -1.0
    )
    key_gradient = apply_rotary(key_gradient, row_pos, -1.0)
    gradients = jnp.concatenate(
        [
            query_gradient.reshape(tok_rows, q_width),
            key_gradient.reshape(tok_rows, kv_width),
            value_gradient.reshape(tok_rows, kv_width),
        ],
        axis=1,
    ).astype(jnp.bfloat16)
    back_gradients = exchange(to_owner_slots(gradients))
    local_attended = from_slots(back_attended)
    local_gradients = from_slots(back_gradients)

    return sum_products(
        input_t,
        cotangent_t,
        weights,
        local_gradients,
        local_attended,
        sources,
        q_width,
        kv_width,
    )


def solution(mesh):
    return jax.shard_map(
        on_device,
        mesh=mesh,
        in_specs=(
            P("ctx", None),
            P(None, "tp"),
            P(None, "tp"),
            P(None, "tp"),
            P(None, "tp"),
            P("ctx", None),
            P(),
            P(),
            P(),
        ),
        out_specs=(P("ctx", "tp"), P("ctx", "tp"), P("ctx", "tp"), P("ctx", "tp"), P("ctx", "tp")),
        check_vma=False,
    )
```

```python
import functools
import math

import jax
import jax.numpy as jnp
from jax import lax
from jax.experimental import pallas as pl
from jax.experimental.pallas import tpu as pltpu
from jax.sharding import PartitionSpec as P

HEAD_SIZE = 128
PIECE = 8


rope_base = 500000.0
fill_value = -1e30


def apply_rotary(heads, positions, direction):
    half_width = heads.shape[-1] // 2
    frequency = rope_base ** (-2.0 * jnp.arange(half_width, dtype=jnp.float32) / heads.shape[-1])
    angles = positions.astype(jnp.float32)[:, None] * frequency[None, :]
    cosine = jnp.cos(angles)[:, None, :]
    sine_term = direction * jnp.sin(angles)[:, None, :]
    lower_half = heads[..., :half_width]
    upper_half = heads[..., half_width:]
    return jnp.concatenate(
        [
            lower_half * cosine - upper_half * sine_term,
            upper_half * cosine + lower_half * sine_term,
        ],
        axis=-1,
    )


def mask_of(query_doc, query_pos, key_doc, key_pos):
    return (query_doc[:, None] == key_doc[None, :]) & (key_pos[None, :] <= query_pos[:, None])


def attend_both(query_matrix, key_heads, value_heads, out_grads, allowed, score_scale):
    scores = (
        jnp.einsum("bkgd,mkd->kgbm", query_matrix, key_heads, preferred_element_type=jnp.float32)
        * score_scale
    )
    scores = jnp.where(allowed, scores, fill_value)
    row_max = jnp.max(scores, axis=-1, keepdims=True)
    exponent = jnp.where(allowed, jnp.exp(scores - row_max), 0.0)
    row_sum = jnp.sum(exponent, axis=-1, keepdims=True)
    probability = exponent / row_sum
    rounded = probability.astype(jnp.bfloat16)
    attended = jnp.einsum(
        "kgbm,mkd->bkgd", rounded, value_heads, preferred_element_type=jnp.float32
    ).astype(jnp.bfloat16)
    row_delta = jnp.einsum(
        "bkgd,bkgd->kgb", out_grads.astype(jnp.float32), attended.astype(jnp.float32)
    )
    prob_grad = jnp.einsum(
        "bkgd,mkd->kgbm", out_grads, value_heads, preferred_element_type=jnp.float32
    )
    score_grad = (probability * (prob_grad - row_delta[..., None])).astype(jnp.bfloat16)
    query_gradient = (
        jnp.einsum("kgbm,mkd->bkgd", score_grad, key_heads, preferred_element_type=jnp.float32)
        * score_scale
    )
    key_gradient = (
        jnp.einsum("kgbm,bkgd->mkd", score_grad, query_matrix, preferred_element_type=jnp.float32)
        * score_scale
    )
    value_gradient = jnp.einsum(
        "kgbm,bkgd->mkd", rounded, out_grads, preferred_element_type=jnp.float32
    )
    return attended, query_gradient, key_gradient, value_gradient


def contract_rows(left, right):
    return lax.dot_general(
        left, right, (((0,), (0,)), ((), ())), preferred_element_type=jnp.float32
    )


def contract_cols(left, right):
    return lax.dot_general(
        left, right, (((1,), (1,)), ((), ())), preferred_element_type=jnp.float32
    )


def spot_of(device, count):
    odd = lax.rem(device, 2)
    half = lax.div(device, 2)
    return (1 - odd) * half + odd * (count - 1 - half)


def device_at(spot, count):
    high = lax.div(spot, count // 2)
    return (1 - high) * (2 * spot) + high * (2 * (count - 1 - spot) + 1)


def sums_kernel(
    count,
    q_width,
    kv_width,
    input_t,
    cotangent_t,
    weights,
    gradients,
    attended,
    grad_in,
    grad_query,
    grad_key,
    grad_value,
    grad_out,
    ring0,
    ring1,
    ring2,
    ring3,
    near_sent,
    near_got,
    far_sent,
    far_got,
    ring_send,
    ring_recv,
    tp_send,
    tp_recv,
):
    me = lax.axis_index("ctx")
    tp = lax.axis_index("tp")
    here = spot_of(me, count)
    after = device_at(lax.rem(here + 1, count), count)
    before = device_at(lax.rem(here + count - 1, count), count)
    low_bit = lax.rem(tp, 2)
    high_bit = lax.div(tp, 2)
    near = tp + 1 - 2 * low_bit
    far = tp + 2 - 4 * high_bit
    mesh_id = pl.DeviceIdType.MESH
    barrier = pltpu.get_barrier_semaphore()
    for target in ((after, tp), (before, tp), (me, near), (me, far)):
        pl.semaphore_signal(barrier, inc=1, device_id=target, device_id_type=mesh_id)
    pl.semaphore_wait(barrier, 4)

    block_rows = input_t.shape[0] // count
    half_grad = gradients.shape[1] // 2
    half_out = attended.shape[1] // 2
    rings = (
        (ring0, input_t, gradients, 0, half_grad, 1),
        (ring1, input_t, gradients, half_grad, half_grad, -1),
        (ring2, cotangent_t, attended, 0, half_out, 1),
        (ring3, cotangent_t, attended, half_out, half_out, -1),
    )

    def term(ring, hop):
        _, left, right, start, width, step = rings[ring]
        if step > 0:
            spot = lax.rem(here + 2 * count - 1 - hop, count)
        else:
            spot = lax.rem(here + 1 + hop, count)
        row = pl.multiple_of(device_at(spot, count) * block_rows, block_rows)
        return jnp.dot(
            left[pl.ds(row, block_rows), :],
            right[:, start : start + width],
            preferred_element_type=jnp.float32,
        )

    def ring_copy(ring, hop):
        buffer = rings[ring][0]
        return pltpu.make_async_remote_copy(
            src_ref=buffer.at[hop],
            dst_ref=buffer.at[hop + 1],
            send_sem=ring_send.at[ring, hop],
            recv_sem=ring_recv.at[ring, hop],
            device_id=(after if rings[ring][5] > 0 else before, tp),
            device_id_type=mesh_id,
        )

    for ring in range(4):
        rings[ring][0][0] = term(ring, 0).astype(jnp.bfloat16)
        ring_copy(ring, 0).start()

    def input_term(chunk):
        rows = grad_in.shape[1]
        row = pl.multiple_of(chunk * rows, rows)
        return lax.dot_general(
            gradients[...],
            weights[pl.ds(row, rows), :],
            (((1,), (1,)), ((), ())),
            preferred_element_type=jnp.float32,
        )

    def near_copy(slot):
        return pltpu.make_async_remote_copy(
            src_ref=near_sent.at[slot],
            dst_ref=near_got.at[slot],
            send_sem=tp_send.at[slot],
            recv_sem=tp_recv.at[slot],
            device_id=(me, near),
            device_id_type=mesh_id,
        )

    far_copy = pltpu.make_async_remote_copy(
        src_ref=far_sent,
        dst_ref=far_got,
        send_sem=tp_send.at[2],
        recv_sem=tp_recv.at[2],
        device_id=(me, far),
        device_id_type=mesh_id,
    )

    near_sent[0] = input_term(2 * (1 - high_bit) + 1 - low_bit).astype(jnp.bfloat16)
    near_copy(0).start()
    near_sent[1] = input_term(2 * high_bit + 1 - low_bit).astype(jnp.bfloat16)
    near_copy(1).start()

    def ring_hop(hop, carry):
        for ring in range(4):
            product = term(ring, hop)
            ring_copy(ring, hop - 1).wait_recv()
            buffer = rings[ring][0]
            total = product + buffer[hop].astype(jnp.float32)
            buffer[hop] = total.astype(jnp.bfloat16)
            ring_copy(ring, hop).start()
        return carry

    early = min(2, count - 1)
    lax.fori_loop(1, early, ring_hop, 0)
    near_copy(0).wait_recv()
    far_sent[...] = (
        input_term(2 * (1 - high_bit) + low_bit) + near_got[0].astype(jnp.float32)
    ).astype(jnp.bfloat16)
    far_copy.start()
    lax.fori_loop(early, count - 1, ring_hop, 0)

    near_copy(1).wait_recv()
    far_copy.wait_recv()
    grad_in[...] = (
        input_term(2 * high_bit + low_bit)
        + near_got[1].astype(jnp.float32)
        + far_got[...].astype(jnp.float32)
    ).astype(jnp.bfloat16)

    pieces = (
        (grad_query, 0, q_width),
        (grad_key, q_width, kv_width),
        (grad_value, q_width + kv_width, kv_width),
    )
    for ring in range(4):
        ring_copy(ring, count - 2).wait_recv()
        buffer, _, right, start, width, _ = rings[ring]
        total = term(ring, count - 1) + buffer[count - 1].astype(jnp.float32)
        total = total.astype(jnp.bfloat16)
        if right is attended:
            grad_out[:, start : start + width] = total
        else:
            for target, low, size in pieces:
                first, last = max(low, start), min(low + size, start + width)
                if first < last:
                    target[:, first - low : last - low] = total[:, first - start : last - start]

    def drain(hop, carry):
        for ring in range(4):
            ring_copy(ring, hop).wait_send()
        return carry

    lax.fori_loop(0, count - 1, drain, 0)
    near_copy(0).wait_send()
    near_copy(1).wait_send()
    far_copy.wait_send()


def sum_products(input_t, cotangent_t, weights, gradients, attended, count, q_width, kv_width):
    model_width, tok_rows = input_t.shape
    block_rows = model_width // count
    in_width = model_width // 4
    half_grad = gradients.shape[1] // 2
    half_out = attended.shape[1] // 2
    half = jnp.bfloat16
    flops = 2 * tok_rows * model_width * (2 * gradients.shape[1] + attended.shape[1])
    vmem = pl.BlockSpec(memory_space=pltpu.VMEM)
    return pl.pallas_call(
        functools.partial(sums_kernel, count, q_width, kv_width),
        out_shape=(
            jax.ShapeDtypeStruct((tok_rows, in_width), half),
            jax.ShapeDtypeStruct((block_rows, q_width), half),
            jax.ShapeDtypeStruct((block_rows, kv_width), half),
            jax.ShapeDtypeStruct((block_rows, kv_width), half),
            jax.ShapeDtypeStruct((block_rows, q_width), half),
        ),
        in_specs=[vmem] * 5,
        out_specs=(vmem,) * 5,
        scratch_shapes=[
            pltpu.VMEM((count, block_rows, half_grad), half),
            pltpu.VMEM((count, block_rows, half_grad), half),
            pltpu.VMEM((count, block_rows, half_out), half),
            pltpu.VMEM((count, block_rows, half_out), half),
            pltpu.VMEM((2, tok_rows, in_width), half),
            pltpu.VMEM((2, tok_rows, in_width), half),
            pltpu.VMEM((tok_rows, in_width), half),
            pltpu.VMEM((tok_rows, in_width), half),
            pltpu.SemaphoreType.DMA((4, count - 1)),
            pltpu.SemaphoreType.DMA((4, count - 1)),
            pltpu.SemaphoreType.DMA((3,)),
            pltpu.SemaphoreType.DMA((3,)),
        ],
        compiler_params=pltpu.CompilerParams(
            collective_id=0, has_side_effects=True, vmem_limit_bytes=56 * 1024 * 1024
        ),
        cost_estimate=pl.CostEstimate(
            flops=flops, bytes_accessed=30 * model_width * tok_rows, transcendentals=0
        ),
    )(input_t, cotangent_t, weights, gradients, attended)


def on_device(
    normed_input,
    w_query,
    key_weight,
    value_weight,
    output_weight,
    output_cotangent,
    piece_doc,
    piece_offset,
    doc_owner,
):
    sources = lax.axis_size("ctx")
    self_index = lax.axis_index("ctx")
    tok_rows = normed_input.shape[0]
    local_q = w_query.shape[1] // HEAD_SIZE
    local_kv = key_weight.shape[1] // HEAD_SIZE
    group_width = local_q // local_kv
    q_width = w_query.shape[1]
    kv_width = key_weight.shape[1]
    per_device = tok_rows // PIECE
    slot_rows = 2 * tok_rows // sources
    per_slot = slot_rows // PIECE
    owner_rows = sources * slot_rows
    score_scale = 1.0 / math.sqrt(HEAD_SIZE)
    within = jnp.arange(PIECE, dtype=jnp.int32)
    doc_ids = jnp.arange(doc_owner.shape[0], dtype=jnp.int32)
    piece_owner = jnp.sum(
        jnp.where(piece_doc[:, None] == doc_ids[None, :], doc_owner[None, :], 0), axis=1
    )
    own_owner = lax.dynamic_slice_in_dim(piece_owner, self_index * per_device, per_device)
    own_offset = lax.dynamic_slice_in_dim(piece_offset, self_index * per_device, per_device)
    own_pos = (own_offset[:, None] + within[None, :]).reshape(-1)
    piece_ids = jnp.arange(per_device, dtype=jnp.int32)
    earlier = (own_owner[:, None] == own_owner[None, :]) & (piece_ids[None, :] < piece_ids[:, None])
    own_rank = jnp.sum(earlier.astype(jnp.int32), axis=1)
    own_slot = own_owner * per_slot + own_rank
    own_row = (own_slot[:, None] * PIECE + within[None, :]).reshape(-1)
    placing = (jnp.arange(owner_rows, dtype=jnp.int32)[:, None] == own_row[None, :]).astype(
        jnp.bfloat16
    )

    def to_slots(matrix):
        return jnp.dot(placing, matrix, preferred_element_type=jnp.float32).astype(jnp.bfloat16)

    def from_slots(matrix):
        return contract_rows(placing, matrix).astype(jnp.bfloat16)

    def exchange(matrix):
        return lax.all_to_all(matrix, "ctx", split_axis=0, concat_axis=0, tiled=True)

    grad_rows = jnp.dot(output_cotangent, output_weight, preferred_element_type=jnp.float32).astype(
        jnp.bfloat16
    )
    got_grad = exchange(to_slots(grad_rows))
    query_rows = apply_rotary(
        jnp.dot(normed_input, w_query, preferred_element_type=jnp.float32).reshape(
            tok_rows, local_q, HEAD_SIZE
        ),
        own_pos,
        1.0,
    )
    query_rows = query_rows.astype(jnp.bfloat16).reshape(tok_rows, q_width)
    all_ids = jnp.arange(piece_owner.shape[0], dtype=jnp.int32)
    mine = piece_owner == self_index
    preceding = mine[None, :] & (all_ids[None, :] < all_ids[:, None])
    same_source = (all_ids[None, :] // per_device) == (all_ids[:, None] // per_device)
    live_rank = jnp.sum(preceding.astype(jnp.int32), axis=1)
    source_rank = jnp.sum((preceding & same_source).astype(jnp.int32), axis=1)
    choosing = mine[None, :] & (live_rank[None, :] == piece_ids[:, None])

    def choose(table):
        return jnp.sum(jnp.where(choosing, table[None, :], 0), axis=1)

    compact_slot = choose(all_ids // per_device * per_slot + source_rank)
    compact_row = (compact_slot[:, None] * PIECE + within[None, :]).reshape(-1)
    packing = (
        jnp.arange(owner_rows, dtype=jnp.int32)[None, :] == compact_row[:, None]
    ).astype(jnp.bfloat16)
    row_doc = jnp.repeat(choose(piece_doc), PIECE)
    row_pos = (choose(piece_offset)[:, None] + within[None, :]).reshape(-1)
    pair_weights = jnp.concatenate([key_weight, value_weight], axis=1)
    weights = jnp.concatenate([w_query, pair_weights], axis=1)
    input_t = normed_input.T
    cotangent_t = output_cotangent.T
    pair_rows = jnp.dot(normed_input, pair_weights, preferred_element_type=jnp.float32)
    key_rows = apply_rotary(
        pair_rows[:, :kv_width].reshape(tok_rows, local_kv, HEAD_SIZE), own_pos, 1.0
    )
    key_rows = key_rows.reshape(tok_rows, kv_width)
    sent_rows = jnp.concatenate(
        [
            query_rows,
            key_rows.astype(jnp.bfloat16),
            pair_rows[:, kv_width:].astype(jnp.bfloat16),
        ],
        axis=1,
    )
    got_rows = exchange(to_slots(sent_rows))

    def to_live(matrix):
        return jnp.dot(packing, matrix, preferred_element_type=jnp.float32).astype(jnp.bfloat16)

    def to_owner_slots(matrix):
        return contract_rows(packing, matrix).astype(jnp.bfloat16)

    live_rows = to_live(got_rows)
    attended, query_gradient, key_gradient, value_gradient = attend_both(
        live_rows[:, :q_width].reshape(tok_rows, local_kv, group_width, HEAD_SIZE),
        live_rows[:, q_width : q_width + kv_width].reshape(tok_rows, local_kv, HEAD_SIZE),
        live_rows[:, q_width + kv_width :].reshape(tok_rows, local_kv, HEAD_SIZE),
        to_live(got_grad).reshape(tok_rows, local_kv, group_width, HEAD_SIZE),
        mask_of(row_doc, row_pos, row_doc, row_pos),
        score_scale,
    )
    back_attended = exchange(to_owner_slots(attended.reshape(tok_rows, q_width)))
    query_gradient = apply_rotary(
        query_gradient.reshape(tok_rows, local_q, HEAD_SIZE), row_pos, -1.0
    )
    key_gradient = apply_rotary(key_gradient, row_pos, -1.0)
    gradients = jnp.concatenate(
        [
            query_gradient.reshape(tok_rows, q_width),
            key_gradient.reshape(tok_rows, kv_width),
            value_gradient.reshape(tok_rows, kv_width),
        ],
        axis=1,
    ).astype(jnp.bfloat16)
    back_gradients = exchange(to_owner_slots(gradients))
    local_attended = from_slots(back_attended)
    local_gradients = from_slots(back_gradients)

    return sum_products(
        input_t,
        cotangent_t,
        weights,
        local_gradients,
        local_attended,
        sources,
        q_width,
        kv_width,
    )


def solution(mesh):
    return jax.shard_map(
        on_device,
        mesh=mesh,
        in_specs=(
            P("ctx", None),
            P(None, "tp"),
            P(None, "tp"),
            P(None, "tp"),
            P(None, "tp"),
            P("ctx", None),
            P(),
            P(),
            P(),
        ),
        out_specs=(P("ctx", "tp"), P("ctx", "tp"), P("ctx", "tp"), P("ctx", "tp"), P("ctx", "tp")),
        check_vma=False,
    )
```
